32 devices in a mesh: grp: 4 (over y, x), shard: 8 (over z, core).
Axes of the slice: x: 2, y: 2, z: 4, core: 2. Of those that a mesh axis runs over, the one named last changes fastest.
Arguments:
- src: float32 [512, 1024], P(('grp', 'shard')), may hold values from -64 to 64
- inv_src: float32 [512], P(('grp', 'shard')), may hold values from 5 to 250
- tgt: float32 [4096, 1024], P(('shard', 'grp')), may hold values from -64 to 64
- inv_tgt: float32 [4096], P(('shard', 'grp')), may hold values from 5 to 250
Outputs:
- margin: float32 [512, 4096], P('grp', 'shard')
The draws below stay inside these ranges and needn't reach their ends.
All inputs are finite; a program needn't handle non-finite values.
Results may differ from the reference program's by a relative error of at most 0.00013.
Values sent between devices are 32-bit elements; how exact they have to be, the bound alone decides.
A program may use at most 64 MiB of HBM per device.

```python
import math
import jax
import jax.numpy as jnp
from jax import lax

D = 1024
SOURCES = 512
TARGETS = 4096


def embeddings(key):
    keys = jax.random.split(jax.random.fold_in(key, 11), 2)
    src = jax.random.normal(keys[0], (SOURCES, D), jnp.float32)
    tgt = jax.random.normal(keys[1], (TARGETS, D), jnp.float32)
    return (jnp.clip(src, -64.0, 64.0), jnp.clip(tgt, -64.0, 64.0))


def draw_src(key, part):
    return embeddings(key)[0]


def draw_tgt(key, part):
    return embeddings(key)[1]


def draw_inv_src(key, part):
    rates = jnp.exp(jax.random.uniform(jax.random.fold_in(key, 21), (SOURCES,), jnp.float32, math.log(5.0), math.log(100.0)))
    return rates


def draw_inv_tgt(key, part):
    rates = jnp.exp(jax.random.uniform(jax.random.fold_in(key, 31), (TARGETS,), jnp.float32, math.log(5.0), math.log(100.0)))
    return rates


def setup_inputs(seed: int = 0) -> dict:
    arg_keys = jax.random.split(jax.random.key(seed), 5)
    src = draw_src(jax.random.fold_in(arg_keys[4], 71), 0)
    inv_src = draw_inv_src(jax.random.fold_in(arg_keys[4], 71), 0)
    tgt = draw_tgt(jax.random.fold_in(arg_keys[4], 71), 0)
    inv_tgt = draw_inv_tgt(jax.random.fold_in(arg_keys[4], 71), 0)
    return dict(src=src, inv_src=inv_src, tgt=tgt, inv_tgt=inv_tgt)


def unit_rows(rows):
    return rows * lax.rsqrt(lax.optimization_barrier(jnp.sum(rows * rows, axis=1, keepdims=True)) + 1e-06)

def reference(src, inv_src, tgt, inv_tgt):
    src_unit = unit_rows(src)
    tgt_unit = unit_rows(tgt)
    sims = jnp.dot(src_unit, tgt_unit.T, precision=lax.Precision.HIGHEST, preferred_element_type=jnp.float32)
    row_lse = jax.nn.logsumexp(sims * inv_src[:, None], axis=1) - math.log(TARGETS)
    col_lse = jax.nn.logsumexp(sims * inv_tgt[None, :], axis=0) - math.log(SOURCES)
    scale = 0.5 * (inv_src[:, None] + inv_tgt[None, :])
    return sims * scale - (jnp.logaddexp(row_lse[:, None], col_lse[None, :]) - math.log(2.0))
```

```python
import functools
import math

import jax
import jax.numpy as jnp
from jax import lax
from jax.experimental import pallas as pl
from jax.experimental.pallas import tpu as pltpu
from jax.sharding import PartitionSpec as P

MESH = pl.DeviceIdType.MESH


def split(rows):
    unit = rows * lax.rsqrt(jnp.sum(rows * rows, axis=1, keepdims=True) + 1e-06)
    high = unit.astype(jnp.bfloat16)
    return high, (unit - high.astype(jnp.float32)).astype(jnp.bfloat16)


def kernel(
    G, S, src, inv_src, tgt, inv_tgt, out,
    X, T, TT, XX, CB, C, IS, BV, BM, L, LM, ISM,
    local_sem, z_s, z_r, f_s, f_r, r_s, r_r, sib_s, sib_r, is_s, is_r,
    cos_s, cos_r, b_s, b_r, l_s, l_r,
):
    Z = S // 2
    n, width = src.shape[0], tgt.shape[0]
    height = n * S
    HF, HR = G // 2, (G - 1) // 2
    g, s = lax.axis_index("grp"), lax.axis_index("shard")
    c, z = lax.rem(s, 2), s // 2
    sgn = 1 - 2 * c
    odd = lax.rem(g, 2)
    p = (1 - odd) * (g // 2) + odd * (G - 1 - g // 2)

    def at(r):
        q = lax.rem(p + sgn * r + G, G)
        h = q // (G // 2)
        return (1 - h) * 2 * q + h * (2 * (G - 1 - q) + 1)

    ahead = [at(r) for r in range(G)]
    zs = [z] + [jnp.bitwise_xor(z, k) for k in range(1, Z)]
    sib = s + 1 - 2 * c

    def rows(group, k, core):
        return pl.ds(pl.multiple_of((group * S + zs[k] * 2 + core) * n, n), n)

    def send(a, b, ss, rs, dev):
        cp = pltpu.make_async_remote_copy(a, b, ss, rs, device_id=dev, device_id_type=MESH)
        cp.start()
        sends.append(cp)

    def arrived(b, rs):
        pltpu.make_async_copy(b, b, rs).wait()

    sends = []
    tcopy = pltpu.make_async_copy(tgt, T, local_sem.at[0])
    tcopy.start()
    own = X.at[rows(g, 0, c)]
    scopy = pltpu.make_async_copy(src, own, local_sem.at[1])
    scopy.start()

    barrier = pltpu.get_barrier_semaphore()
    for d in range(1, S):
        pl.semaphore_signal(barrier, inc=1, device_id=(g, lax.rem(s + d, S)), device_id_type=MESH)
    for r in range(1, G):
        pl.semaphore_signal(barrier, inc=1, device_id=(ahead[r], s), device_id_type=MESH)
    pl.semaphore_wait(barrier, S + G - 2)

    for k in range(1, Z):
        send(src, own, z_s.at[k], z_r.at[k], (g, zs[k] * 2 + c))

    fwd, back = (ahead[1], s), (ahead[G - 1], s)

    def onward(piece, where, k, hop, stream):
        if stream != "r" and hop < HF:
            send(piece, where, f_s.at[hop, k], f_r.at[hop, k], fwd)
        if stream != "f" and hop < HR:
            send(piece, where, r_s.at[hop, k], r_r.at[hop, k], back)
        i = hop if stream != "r" else HF + hop
        send(piece, where, sib_s.at[i, k], sib_r.at[i, k], (g, sib))

    def prepare(group, k, i_sib):
        arrived(X.at[rows(group, k, 1 - c)], sib_r.at[i_sib, k])
        at_row = pl.multiple_of((group * S + zs[k] * 2) * n, 2 * n)
        to_row = pl.multiple_of(zs[k] * 2 * n, 2 * n)
        high, low = split(X[pl.ds(at_row, 2 * n), :])
        XX[pl.ds(to_row, 2 * n), :] = high
        XX[pl.ds(height + to_row, 2 * n), :] = low

    def block():
        w = lax.dot_general(
            XX[...], TT[...], (((1,), (1,)), ((), ())), preferred_element_type=jnp.float32
        )
        return (w[:height, :width] + (w[:height, width:] + w[height:, :width]))

    state = [None]

    def column(cos):
        logits = cos * inv_tgt[...]
        top = jnp.max(logits, axis=0, keepdims=True)
        if state[0] is not None:
            top = jnp.maximum(top, state[0][0])
        total = jnp.sum(jnp.exp(logits - top), axis=0, keepdims=True)
        if state[0] is not None:
            total = total + state[0][1] * jnp.exp(state[0][0] - top)
        state[0] = (top, total)

    def finish(r):
        cos = block()
        if r == 0:
            C[g] = cos
        else:
            CB[r - 1] = cos
            send(CB.at[r - 1], C.at[g], cos_s.at[r - 1], cos_r.at[r - 1], (ahead[r], s))
        column(cos)

    for t in range(Z + HF):
        for h in range(HF, -1, -1):
            k = t - h
            if not 0 <= k < Z:
                continue
            if h == 0:
                if k == 0:
                    onward(src, own, 0, 0, "own")
                else:
                    where = X.at[rows(g, k, c)]
                    arrived(where, z_r.at[k])
                    onward(where, where, k, 0, "own")
                continue
            where = X.at[rows(ahead[G - h], k, c)]
            arrived(where, f_r.at[h - 1, k])
            onward(where, where, k, h, "f")
            if h <= HR:
                where = X.at[rows(ahead[h], k, c)]
                arrived(where, r_r.at[h - 1, k])
                onward(where, where, k, h, "r")
        if t == 0:
            lane = lax.broadcasted_iota(jnp.int32, (n, n), 1)
            sub = lax.broadcasted_iota(jnp.int32, (n, n), 0)
            column_inv = jnp.sum(
                jnp.where(lane == sub, jnp.broadcast_to(inv_src[...], (n, n)), 0.0),
                axis=1, keepdims=True,
            )
            ISM[...] = jnp.broadcast_to(column_inv, (n, 128))
            mine = pl.ds(pl.multiple_of(s * n, n), n)
            IS[mine, :] = ISM[...]
            for d in range(1, S):
                send(ISM, IS.at[mine, :], is_s.at[d], is_r.at[d], (g, lax.rem(s + d, S)))
            tcopy.wait()
            for i in range(0, width, 32):
                high, low = split(T[i : i + 32, :])
                TT[i : i + 32, :] = high
                TT[width + i : width + i + 32, :] = low
            scopy.wait()
        if 1 <= t <= Z:
            prepare(g, t - 1, 0)
        if t == Z:
            finish(0)

    for h in range(1, HF + 1):
        if h <= HR:
            for k in range(Z):
                prepare(ahead[G - h], k, HF + h)
            finish(G - h)
        for k in range(Z):
            prepare(ahead[h], k, h)
        finish(h)

    top, total = state[0]
    b = top + jnp.log(total) - math.log(height * G)
    BM[0:1, :] = b
    BM[1:2, :] = inv_tgt[...]
    BV[g] = BM[...]
    for r in range(1, G):
        send(BM, BV.at[g], b_s.at[r], b_r.at[r], (ahead[r], s))

    for d in range(1, S):
        frm = lax.rem(s + S - d, S)
        arrived(IS.at[pl.ds(pl.multiple_of(frm * n, n), n), :], is_r.at[d])
    for r in range(1, G):
        arrived(C.at[ahead[G - r]], cos_r.at[r - 1])

    inv_rows = IS[...]
    logits = [C[j] * inv_rows for j in range(G)]
    top = functools.reduce(jnp.maximum, logits)
    top = jnp.max(top, axis=1, keepdims=True)
    total = jnp.sum(sum(jnp.exp(x - top) for x in logits), axis=1, keepdims=True)
    part = top + jnp.log(total)
    LM[...] = jnp.transpose(jnp.broadcast_to(part, (height, 128)))[:8, :]
    L[s] = LM[...]
    for d in range(1, S):
        send(LM, L.at[s], l_s.at[d], l_r.at[d], (g, lax.rem(s + d, S)))
    for r in range(1, G):
        arrived(BV.at[ahead[G - r]], b_r.at[r])
    for d in range(1, S):
        arrived(L.at[lax.rem(s + S - d, S)], l_r.at[d])

    parts = L[...]
    top = jnp.max(parts, axis=0)
    a = top + jnp.log(jnp.sum(jnp.exp(parts - top[None]), axis=0)) - math.log(G * width * S)
    a = jnp.transpose(jnp.broadcast_to(a[:1, :], (128, height)))
    for j in range(G):
        b = BV[j, 0:1, :]
        scale = 0.5 * (inv_rows + BV[j, 1:2, :])
        both = jnp.maximum(a, b) + jnp.log(1.0 + jnp.exp(-jnp.abs(a - b)))
        out[:, j * width : (j + 1) * width] = C[j] * scale - (both - math.log(2.0))

    for cp in sends:
        cp.wait_send()


def body(src, inv_src, tgt, inv_tgt):
    G, S = lax.axis_size("grp"), lax.axis_size("shard")
    n, depth = src.shape
    width = tgt.shape[0]
    height = n * S
    Z, HF, HR = S // 2, G // 2, (G - 1) // 2
    f32, bf16 = jnp.float32, jnp.bfloat16
    dma = pltpu.SemaphoreType.DMA
    vmem = pl.BlockSpec(memory_space=pltpu.VMEM)
    anyw = pl.BlockSpec(memory_space=pl.ANY)
    return pl.pallas_call(
        functools.partial(kernel, G, S),
        out_shape=jax.ShapeDtypeStruct((height, G * width), f32),
        in_specs=[anyw, vmem, anyw, vmem],
        out_specs=vmem,
        scratch_shapes=[
            pltpu.VMEM((G * height, depth), f32),
            pltpu.VMEM((width, depth), f32),
            pltpu.VMEM((2 * width, depth), bf16),
            pltpu.VMEM((2 * height, depth), bf16),
            pltpu.VMEM((G - 1, height, width), f32),
            pltpu.VMEM((G, height, width), f32),
            pltpu.VMEM((height, 128), f32),
            pltpu.VMEM((G, 8, width), f32),
            pltpu.VMEM((8, width), f32),
            pltpu.VMEM((S, 8, height), f32),
            pltpu.VMEM((8, height), f32),
            pltpu.VMEM((n, 128), f32),
            dma((2,)),
            dma((Z,)), dma((Z,)),
            dma((HF, Z)), dma((HF, Z)),
            dma((HR, Z)), dma((HR, Z)),
            dma((HF + HR + 1, Z)), dma((HF + HR + 1, Z)),
            dma((S,)), dma((S,)),
            dma((G - 1,)), dma((G - 1,)),
            dma((G,)), dma((G,)),
            dma((S,)), dma((S,)),
        ],
        compiler_params=pltpu.CompilerParams(
            collective_id=0, has_side_effects=True, vmem_limit_bytes=56 * 2**20
        ),
        cost_estimate=pl.CostEstimate(
            flops=8 * G * height * width * depth, bytes_accessed=8 * width * depth,
            transcendentals=4 * G * height * width,
        ),
    )(src, inv_src.reshape(1, n), tgt, inv_tgt.reshape(1, width))


def solution(mesh):
    return jax.shard_map(
        body,
        mesh=mesh,
        in_specs=(
            P(("grp", "shard"), None),
            P(("grp", "shard")),
            P(("shard", "grp"), None),
            P(("shard", "grp")),
        ),
        out_specs=P("grp", "shard"),
        check_vma=False,
    )
```

```python
import functools
import math

import jax
import jax.numpy as jnp
from jax import lax
from jax.experimental import pallas as pl
from jax.experimental.pallas import tpu as pltpu
from jax.sharding import PartitionSpec as P

MESH = pl.DeviceIdType.MESH


def split(rows):
    unit = rows * lax.rsqrt(jnp.sum(rows * rows, axis=1, keepdims=True) + 1e-06)
    high = unit.astype(jnp.bfloat16)
    return high, (unit - high.astype(jnp.float32)).astype(jnp.bfloat16)


def kernel(
    G, S, src, inv_src, tgt, inv_tgt, out,
    X, T, TT, XX, TI, CB, C, IS, ISM, BM, BV, LM, L,
    local_sem, t_s, t_r, z_s, z_r, f_s, f_r, r_s, r_r, is_s, is_r,
    cos_s, cos_r, b_s, b_r, l_s, l_r,
):
    Z = S // 2
    n, width = src.shape[0], tgt.shape[0]
    half = n * Z
    height = n * S
    HF, HR = G // 2, (G - 1) // 2
    g, s = lax.axis_index("grp"), lax.axis_index("shard")
    c, z = lax.rem(s, 2), s // 2
    sgn = 1 - 2 * c
    odd = lax.rem(g, 2)
    p = (1 - odd) * (g // 2) + odd * (G - 1 - g // 2)

    def at(r):
        q = lax.rem(p + sgn * r + G, G)
        h = q // (G // 2)
        return (1 - h) * 2 * q + h * (2 * (G - 1 - q) + 1)

    ahead = [at(r) for r in range(G)]
    zs = [z] + [jnp.bitwise_xor(z, k) for k in range(1, Z)]
    other = 1 - c
    sib = z * 2 + other

    def rows(k):
        return pl.ds(pl.multiple_of(zs[k] * n, n), n)

    def send(a, b, ss, rs, dev):
        cp = pltpu.make_async_remote_copy(a, b, ss, rs, device_id=dev, device_id_type=MESH)
        cp.start()
        sends.append(cp)

    def arrived(b, rs):
        pltpu.make_async_copy(b, b, rs).wait()

    def signal(dev):
        pl.semaphore_signal(barrier, inc=1, device_id=dev, device_id_type=MESH)

    sends = []
    barrier = pltpu.get_barrier_semaphore()
    for d in range(1, S):
        signal((g, lax.rem(s + d, S)))
    for r in range(1, G):
        for o in range(2):
            signal((ahead[r], z * 2 + o))
    mine_t = pl.ds(pl.multiple_of(c * width, width), width)
    their_t = pl.ds(pl.multiple_of(other * width, width), width)
    tcopy = pltpu.make_async_copy(tgt, T.at[mine_t, :], local_sem.at[0])
    tcopy.start()
    scopy = pltpu.make_async_copy(src, X.at[g, rows(0), :], local_sem.at[1])
    scopy.start()
    TI[c] = jnp.broadcast_to(inv_tgt[...], (8, width))
    pl.semaphore_wait(barrier, S - 1 + 2 * (G - 1))

    for k in range(1, Z):
        send(src, X.at[g, rows(0), :], z_s.at[k], z_r.at[k], (g, zs[k] * 2 + c))

    fwd, back = (ahead[1], s), (ahead[G - 1], s)

    def onward(piece, where, k, hop, stream):
        if stream != "r" and hop < HF:
            send(piece, where, f_s.at[hop, k], f_r.at[hop, k], fwd)
        if stream != "f" and hop < HR:
            send(piece, where, r_s.at[hop, k], r_r.at[hop, k], back)

    def prepare(r, k):
        high, low = split(X[ahead[r], rows(k), :])
        XX[r, rows(k), :] = high
        XX[r, pl.ds(pl.multiple_of(half + zs[k] * n, n), n), :] = low

    state = [None, None]

    def column(o, cos):
        logits = cos * TI[o, 0:1, :]
        top = jnp.max(logits, axis=0, keepdims=True)
        if state[o] is not None:
            top = jnp.maximum(top, state[o][0])
        total = jnp.sum(jnp.exp(logits - top), axis=0, keepdims=True)
        if state[o] is not None:
            total = total + state[o][1] * jnp.exp(state[o][0] - top)
        state[o] = (top, total)

    def finish(r):
        w = lax.dot_general(
            XX[r], TT[...], (((1,), (1,)), ((), ())), preferred_element_type=jnp.float32
        )
        cos = w[:half, : 2 * width] + (w[:half, 2 * width :] + w[half:, : 2 * width])
        parts = [cos[:, o * width : (o + 1) * width] for o in range(2)]
        for o in range(2):
            CB[r, o] = parts[o]
            if r > 0:
                send(CB.at[r, o], C.at[g, c], cos_s.at[r, o], cos_r.at[r, c], (ahead[r], z * 2 + o))
        if r == 0:
            C[g, c] = CB[0, c]
            send(CB.at[0, other], C.at[g, c], cos_s.at[0, 0], cos_r.at[0, c], (g, sib))
        for o in range(2):
            column(o, parts[o])

    def targets(o):
        for i in range(0, width, 32):
            high, low = split(T[pl.ds(pl.multiple_of(o * width + i, 32), 32), :])
            TT[pl.ds(pl.multiple_of(o * width + i, 32), 32), :] = high
            TT[pl.ds(pl.multiple_of((2 + o) * width + i, 32), 32), :] = low

    for t in range(Z + HF):
        ready = []
        for h in range(HF, -1, -1):
            k = t - h
            if not 0 <= k < Z:
                continue
            if h == 0:
                where = X.at[g, rows(k), :]
                if k == 0:
                    onward(src, where, 0, 0, "own")
                else:
                    arrived(where, z_r.at[k])
                    onward(where, where, k, 0, "own")
                    ready.append((0, k))
                continue
            where = X.at[ahead[G - h], rows(k), :]
            arrived(where, f_r.at[h - 1, k])
            onward(where, where, k, h, "f")
            ready.append((G - h, k))
            if h <= HR:
                where = X.at[ahead[h], rows(k), :]
                arrived(where, r_r.at[h - 1, k])
                onward(where, where, k, h, "r")
                ready.append((h, k))
        if t == 0:
            send(tgt, T.at[mine_t, :], t_s.at[0], t_r.at[0], (g, sib))
            send(TI.at[c], TI.at[c], t_s.at[1], t_r.at[1], (g, sib))
            lane = lax.broadcasted_iota(jnp.int32, (n, n), 1)
            sub = lax.broadcasted_iota(jnp.int32, (n, n), 0)
            column_inv = jnp.sum(
                jnp.where(lane == sub, jnp.broadcast_to(inv_src[...], (n, n)), 0.0),
                axis=1, keepdims=True,
            )
            ISM[...] = jnp.broadcast_to(column_inv, (n, 128))
            IS[c, rows(0), :] = ISM[...]
            for d in range(1, S):
                send(ISM, IS.at[c, rows(0), :], is_s.at[d], is_r.at[d], (g, lax.rem(s + d, S)))
            scopy.wait()
            prepare(0, 0)
            tcopy.wait()
            targets(c)
        if t == 1:
            arrived(T.at[their_t, :], t_r.at[0])
            arrived(TI.at[other], t_r.at[1])
            targets(other)
        for r, k in ready:
            prepare(r, k)
            if k == Z - 1:
                finish(r)

    for o in range(2):
        top, total = state[o]
        BM[o] = TI[o]
        BM[o, 0:1, :] = top + jnp.log(total)
    BV[g, c] = BM[c]
    send(BM.at[other], BV.at[g, c], b_s.at[0, 0], b_r.at[0, c], (g, sib))
    for r in range(1, G):
        for o in range(2):
            send(BM.at[o], BV.at[g, c], b_s.at[r, o], b_r.at[r, c], (ahead[r], z * 2 + o))

    for d in range(1, S):
        frm = lax.rem(s + S - d, S)
        place = pl.ds(pl.multiple_of(frm // 2 * n, n), n)
        arrived(IS.at[lax.rem(frm, 2), place, :], is_r.at[d])

    froms = [(g, other, 0)]
    for r in range(1, G):
        froms += [(ahead[G - r], c, r), (ahead[r], other, r)]
    for group, core, r in froms:
        arrived(C.at[group, core], cos_r.at[r, core])

    inv_rows = IS[...]
    logits = [C[j] * inv_rows for j in range(G)]
    top = jnp.max(functools.reduce(jnp.maximum, logits), axis=2, keepdims=True)
    total = jnp.sum(sum(jnp.exp(x - top) for x in logits), axis=2, keepdims=True)
    part = (top + jnp.log(total)).reshape(height, 1)
    LM[...] = jnp.transpose(jnp.broadcast_to(part, (height, 128)))[:8, :]
    L[s] = LM[...]
    for d in range(1, S):
        send(LM, L.at[s], l_s.at[d], l_r.at[d], (g, lax.rem(s + d, S)))
    for group, core, r in froms:
        arrived(BV.at[group, core], b_r.at[r, core])
    for d in range(1, S):
        arrived(L.at[lax.rem(s + S - d, S)], l_r.at[d])

    parts = L[...]
    top = jnp.max(parts, axis=0)
    a = top + jnp.log(jnp.sum(jnp.exp(parts - top[None]), axis=0)) - math.log(G * width * S)
    a = jnp.transpose(jnp.broadcast_to(a[:1, :], (128, height))).reshape(2, half, 128)
    for j in range(G):
        first, second = BV[j, 0, 0:1, :], BV[j, 1, 0:1, :]
        b = jnp.maximum(first, second) + jnp.log(1.0 + jnp.exp(-jnp.abs(first - second)))
        b = b - math.log(height * G)
        both = jnp.maximum(a, b) + jnp.log(1.0 + jnp.exp(-jnp.abs(a - b)))
        scale = 0.5 * (inv_rows + BV[j, 0, 1:2, :])
        margin = C[j] * scale - (both - math.log(2.0))
        for o in range(2):
            for q in range(Z):
                place = (q * 2 + o) * n
                out[place : place + n, j * width : (j + 1) * width] = margin[o, q * n : (q + 1) * n]

    for cp in sends:
        cp.wait_send()


def body(src, inv_src, tgt, inv_tgt):
    G, S = lax.axis_size("grp"), lax.axis_size("shard")
    n, depth = src.shape
    width = tgt.shape[0]
    height = n * S
    half = height // 2
    Z, HF, HR = S // 2, G // 2, (G - 1) // 2
    f32, bf16 = jnp.float32, jnp.bfloat16
    dma = pltpu.SemaphoreType.DMA
    vmem = pl.BlockSpec(memory_space=pltpu.VMEM)
    anyw = pl.BlockSpec(memory_space=pl.ANY)
    return pl.pallas_call(
        functools.partial(kernel, G, S),
        out_shape=jax.ShapeDtypeStruct((height, G * width), f32),
        in_specs=[anyw, vmem, anyw, vmem],
        out_specs=vmem,
        scratch_shapes=[
            pltpu.VMEM((G, half, depth), f32),
            pltpu.VMEM((2 * width, depth), f32),
            pltpu.VMEM((4 * width, depth), bf16),
            pltpu.VMEM((G, 2 * half, depth), bf16),
            pltpu.VMEM((2, 8, width), f32),
            pltpu.VMEM((G, 2, half, width), f32),
            pltpu.VMEM((G, 2, half, width), f32),
            pltpu.VMEM((2, half, 128), f32),
            pltpu.VMEM((n, 128), f32),
            pltpu.VMEM((2, 8, width), f32),
            pltpu.VMEM((G, 2, 8, width), f32),
            pltpu.VMEM((8, height), f32),
            pltpu.VMEM((S, 8, height), f32),
            dma((2,)),
            dma((2,)), dma((2,)),
            dma((Z,)), dma((Z,)),
            dma((HF, Z)), dma((HF, Z)),
            dma((HR, Z)), dma((HR, Z)),
            dma((S,)), dma((S,)),
            dma((G, 2)), dma((G, 2)),
            dma((G, 2)), dma((G, 2)),
            dma((S,)), dma((S,)),
        ],
        compiler_params=pltpu.CompilerParams(
            collective_id=0, has_side_effects=True, vmem_limit_bytes=56 * 2**20
        ),
        cost_estimate=pl.CostEstimate(
            flops=8 * G * height * width * depth, bytes_accessed=8 * width * depth,
            transcendentals=4 * G * height * width,
        ),
    )(src, inv_src.reshape(1, n), tgt, inv_tgt.reshape(1, width))


def solution(mesh):
    return jax.shard_map(
        body,
        mesh=mesh,
        in_specs=(
            P(("grp", "shard"), None),
            P(("grp", "shard")),
            P(("shard", "grp"), None),
            P(("shard", "grp")),
        ),
        out_specs=P("grp", "shard"),
        check_vma=False,
    )
```

```python
import functools
import math

import jax
import jax.numpy as jnp
from jax import lax
from jax.experimental import pallas as pl
from jax.experimental.pallas import tpu as pltpu
from jax.sharding import PartitionSpec as P

MESH = pl.DeviceIdType.MESH


def split(rows):
    unit = rows * lax.rsqrt(jnp.sum(rows * rows, axis=1, keepdims=True) + 1e-06)
    high = unit.astype(jnp.bfloat16)
    return high, (unit - high.astype(jnp.float32)).astype(jnp.bfloat16)


def kernel(
    G, S, src, inv_src, tgt, inv_tgt, out,
    X, T, TT, XX, TI, CB, C, IS, ISM, BM, BV, LM, L,
    local_sem, t_s, t_r, z_s, z_r, f_s, f_r, r_s, r_r, is_s, is_r,
    cos_s, cos_r, b_s, b_r, l_s, l_r,
):
    Z = S // 2
    n, width = src.shape[0], tgt.shape[0]
    half = n * Z
    height = n * S
    HF, HR = G // 2, (G - 1) // 2
    g, s = lax.axis_index("grp"), lax.axis_index("shard")
    c, z = lax.rem(s, 2), s // 2
    sgn = 1 - 2 * c
    odd = lax.rem(g, 2)
    p = (1 - odd) * (g // 2) + odd * (G - 1 - g // 2)

    def at(r):
        q = lax.rem(p + sgn * r + G, G)
        h = q // (G // 2)
        return (1 - h) * 2 * q + h * (2 * (G - 1 - q) + 1)

    ahead = [at(r) for r in range(G)]
    order = [0]
    for r in range(1, HF + 1):
        order += [G - r] if G - r == r else [G - r, r]
    zs = [z] + [jnp.bitwise_xor(z, k) for k in range(1, Z)]
    other = 1 - c
    sib = z * 2 + other

    def rows(k):
        return pl.ds(pl.multiple_of(zs[k] * n, n), n)

    def send(a, b, ss, rs, dev):
        cp = pltpu.make_async_remote_copy(a, b, ss, rs, device_id=dev, device_id_type=MESH)
        cp.start()
        sends.append(cp)

    def arrived(b, rs):
        pltpu.make_async_copy(b, b, rs).wait()

    def signal(dev):
        pl.semaphore_signal(barrier, inc=1, device_id=dev, device_id_type=MESH)

    sends = []
    barrier = pltpu.get_barrier_semaphore()
    for d in range(1, S):
        signal((g, lax.rem(s + d, S)))
    for r in range(1, G):
        for o in range(2):
            signal((ahead[r], z * 2 + o))
    mine_t = pl.ds(pl.multiple_of(c * width, width), width)
    tcopy = pltpu.make_async_copy(tgt, T.at[mine_t, :], local_sem.at[0])
    tcopy.start()
    scopy = pltpu.make_async_copy(src, X.at[g, rows(0), :], local_sem.at[1])
    scopy.start()
    TI[c] = jnp.broadcast_to(inv_tgt[...], (8, width))
    pl.semaphore_wait(barrier, S - 1 + 2 * (G - 1))

    for k in range(1, Z):
        send(src, X.at[g, rows(0), :], z_s.at[k], z_r.at[k], (g, zs[k] * 2 + c))

    fwd, back = (ahead[1], s), (ahead[G - 1], s)

    def onward(piece, where, k, hop, stream):
        if stream != "r" and hop < HF:
            send(piece, where, f_s.at[hop, k], f_r.at[hop, k], fwd)
        if stream != "f" and hop < HR:
            send(piece, where, r_s.at[hop, k], r_r.at[hop, k], back)

    def prepare(r, k):
        high, low = split(X[ahead[r], rows(k), :])
        i = order.index(r)
        XX[i, rows(k), :] = high
        XX[i, pl.ds(pl.multiple_of(half + zs[k] * n, n), n), :] = low

    state = [None, None]

    def column(o, cos):
        logits = cos * TI[o, 0:1, :]
        top = jnp.max(logits, axis=0, keepdims=True)
        if state[o] is not None:
            top = jnp.maximum(top, state[o][0])
        total = jnp.sum(jnp.exp(logits - top), axis=0, keepdims=True)
        if state[o] is not None:
            total = total + state[o][1] * jnp.exp(state[o][0] - top)
        state[o] = (top, total)

    def finish(first, last):
        count = last - first
        w = lax.dot_general(
            XX[first:last].reshape(count * 2 * half, XX.shape[2]), TT[...],
            (((1,), (1,)), ((), ())), preferred_element_type=jnp.float32,
        ).reshape(count, 2 * half, 4 * width)
        blocks = []
        for i in range(count):
            r, v = order[first + i], w[i]
            cos = v[:half, : 2 * width] + (v[:half, 2 * width :] + v[half:, : 2 * width])
            parts = [cos[:, o * width : (o + 1) * width] for o in range(2)]
            blocks.append(parts)
            for o in range(2):
                CB[r, o] = parts[o]
                if r > 0:
                    send(
                        CB.at[r, o], C.at[g, c], cos_s.at[r, o], cos_r.at[r, c],
                        (ahead[r], z * 2 + o),
                    )
            if r == 0:
                C[g, c] = CB[0, c]
                send(CB.at[0, other], C.at[g, c], cos_s.at[0, 0], cos_r.at[0, c], (g, sib))
        for parts in blocks:
            for o in range(2):
                column(o, parts[o])

    chunk = width // 4

    def piece_of(o, i):
        return pl.ds(pl.multiple_of(o * width + i * chunk, chunk), chunk)

    def targets(o, i):
        high, low = split(T[piece_of(o, i), :])
        TT[piece_of(o, i), :] = high
        TT[piece_of(o + 2, i), :] = low

    finished = 0
    for t in range(Z + HF):
        ready = []
        for h in range(HF, -1, -1):
            k = t - h
            if not 0 <= k < Z:
                continue
            if h == 0:
                where = X.at[g, rows(k), :]
                if k == 0:
                    onward(src, where, 0, 0, "own")
                else:
                    arrived(where, z_r.at[k])
                    onward(where, where, k, 0, "own")
                    ready.append((0, k))
                continue
            where = X.at[ahead[G - h], rows(k), :]
            arrived(where, f_r.at[h - 1, k])
            onward(where, where, k, h, "f")
            ready.append((G - h, k))
            if h <= HR:
                where = X.at[ahead[h], rows(k), :]
                arrived(where, r_r.at[h - 1, k])
                onward(where, where, k, h, "r")
                ready.append((h, k))
        if t < 4:
            send(
                tgt.at[pl.ds(t * chunk, chunk), :], T.at[piece_of(c, t), :],
                t_s.at[t], t_r.at[t], (g, sib),
            )
        if t == 0:
            send(TI.at[c], TI.at[c], t_s.at[4], t_r.at[4], (g, sib))
            lane = lax.broadcasted_iota(jnp.int32, (n, n), 1)
            sub = lax.broadcasted_iota(jnp.int32, (n, n), 0)
            column_inv = jnp.sum(
                jnp.where(lane == sub, jnp.broadcast_to(inv_src[...], (n, n)), 0.0),
                axis=1, keepdims=True,
            )
            ISM[...] = jnp.broadcast_to(column_inv, (n, 128))
            IS[c, rows(0), :] = ISM[...]
            for d in range(1, S):
                send(ISM, IS.at[c, rows(0), :], is_s.at[d], is_r.at[d], (g, lax.rem(s + d, S)))
            scopy.wait()
            prepare(0, 0)
            tcopy.wait()
            for i in range(4):
                targets(c, i)
        for r, k in ready:
            prepare(r, k)
        if 1 <= t <= 4:
            arrived(T.at[piece_of(other, t - 1), :], t_r.at[t - 1])
            targets(other, t - 1)
        if t == 4:
            arrived(TI.at[other], t_r.at[4])
        if t >= Z:
            done = len([r for r, k in ready if k == Z - 1])
            finish(finished, finished + done + (t == Z))
            finished += done + (t == Z)

    for o in range(2):
        top, total = state[o]
        BM[o] = TI[o]
        BM[o, 0:1, :] = top + jnp.log(total)
    BV[g, c] = BM[c]
    send(BM.at[other], BV.at[g, c], b_s.at[0, 0], b_r.at[0, c], (g, sib))
    for r in range(1, G):
        for o in range(2):
            send(BM.at[o], BV.at[g, c], b_s.at[r, o], b_r.at[r, c], (ahead[r], z * 2 + o))

    for d in range(1, S):
        frm = lax.rem(s + S - d, S)
        place = pl.ds(pl.multiple_of(frm // 2 * n, n), n)
        arrived(IS.at[lax.rem(frm, 2), place, :], is_r.at[d])

    froms = [(g, other, 0)]
    for r in range(1, G):
        froms += [(ahead[G - r], c, r), (ahead[r], other, r)]
    for group, core, r in froms:
        arrived(C.at[group, core], cos_r.at[r, core])

    inv_rows = IS[...]
    logits = [C[j] * inv_rows for j in range(G)]
    top = jnp.max(functools.reduce(jnp.maximum, logits), axis=2, keepdims=True)
    total = jnp.sum(sum(jnp.exp(x - top) for x in logits), axis=2, keepdims=True)
    part = (top + jnp.log(total)).reshape(height, 1)
    LM[...] = jnp.transpose(jnp.broadcast_to(part, (height, 128)))[:8, :]
    L[s] = LM[...]
    for d in range(1, S):
        send(LM, L.at[s], l_s.at[d], l_r.at[d], (g, lax.rem(s + d, S)))
    for group, core, r in froms:
        arrived(BV.at[group, core], b_r.at[r, core])
    for d in range(1, S):
        arrived(L.at[lax.rem(s + S - d, S)], l_r.at[d])

    parts = L[...]
    top = jnp.max(parts, axis=0)
    a = top + jnp.log(jnp.sum(jnp.exp(parts - top[None]), axis=0)) - math.log(G * width * S)
    a = jnp.transpose(jnp.broadcast_to(a[:1, :], (128, height))).reshape(2, half, 128)
    for j in range(G):
        first, second = BV[j, 0, 0:1, :], BV[j, 1, 0:1, :]
        b = jnp.maximum(first, second) + jnp.log(1.0 + jnp.exp(-jnp.abs(first - second)))
        b = b - math.log(height * G)
        both = jnp.maximum(a, b) + jnp.log(1.0 + jnp.exp(-jnp.abs(a - b)))
        scale = 0.5 * (inv_rows + BV[j, 0, 1:2, :])
        margin = C[j] * scale - (both - math.log(2.0))
        for o in range(2):
            for q in range(Z):
                place = (q * 2 + o) * n
                out[place : place + n, j * width : (j + 1) * width] = margin[o, q * n : (q + 1) * n]

    for cp in sends:
        cp.wait_send()


def body(src, inv_src, tgt, inv_tgt):
    G, S = lax.axis_size("grp"), lax.axis_size("shard")
    n, depth = src.shape
    width = tgt.shape[0]
    height = n * S
    half = height // 2
    Z, HF, HR = S // 2, G // 2, (G - 1) // 2
    f32, bf16 = jnp.float32, jnp.bfloat16
    dma = pltpu.SemaphoreType.DMA
    vmem = pl.BlockSpec(memory_space=pltpu.VMEM)
    anyw = pl.BlockSpec(memory_space=pl.ANY)
    return pl.pallas_call(
        functools.partial(kernel, G, S),
        out_shape=jax.ShapeDtypeStruct((height, G * width), f32),
        in_specs=[anyw, vmem, anyw, vmem],
        out_specs=vmem,
        scratch_shapes=[
            pltpu.VMEM((G, half, depth), f32),
            pltpu.VMEM((2 * width, depth), f32),
            pltpu.VMEM((4 * width, depth), bf16),
            pltpu.VMEM((G, 2 * half, depth), bf16),
            pltpu.VMEM((2, 8, width), f32),
            pltpu.VMEM((G, 2, half, width), f32),
            pltpu.VMEM((G, 2, half, width), f32),
            pltpu.VMEM((2, half, 128), f32),
            pltpu.VMEM((n, 128), f32),
            pltpu.VMEM((2, 8, width), f32),
            pltpu.VMEM((G, 2, 8, width), f32),
            pltpu.VMEM((8, height), f32),
            pltpu.VMEM((S, 8, height), f32),
            dma((2,)),
            dma((5,)), dma((5,)),
            dma((Z,)), dma((Z,)),
            dma((HF, Z)), dma((HF, Z)),
            dma((HR, Z)), dma((HR, Z)),
            dma((S,)), dma((S,)),
            dma((G, 2)), dma((G, 2)),
            dma((G, 2)), dma((G, 2)),
            dma((S,)), dma((S,)),
        ],
        compiler_params=pltpu.CompilerParams(
            collective_id=0, has_side_effects=True, vmem_limit_bytes=56 * 2**20
        ),
        cost_estimate=pl.CostEstimate(
            flops=8 * G * height * width * depth, bytes_accessed=8 * width * depth,
            transcendentals=4 * G * height * width,
        ),
    )(src, inv_src.reshape(1, n), tgt, inv_tgt.reshape(1, width))


def solution(mesh):
    return jax.shard_map(
        body,
        mesh=mesh,
        in_specs=(
            P(("grp", "shard"), None),
            P(("grp", "shard")),
            P(("shard", "grp"), None),
            P(("shard", "grp")),
        ),
        out_specs=P("grp", "shard"),
        check_vma=False,
    )
```

```python
import functools
import math

import jax
import jax.numpy as jnp
from jax import lax
from jax.experimental import pallas as pl
from jax.experimental.pallas import tpu as pltpu
from jax.sharding import PartitionSpec as P

MESH = pl.DeviceIdType.MESH


def split(rows):
    unit = rows * lax.rsqrt(jnp.sum(rows * rows, axis=1, keepdims=True) + 1e-06)
    high = unit.astype(jnp.bfloat16)
    return high, (unit - high.astype(jnp.float32)).astype(jnp.bfloat16)


def kernel(
    G, S, src, inv_src, tgt, inv_tgt, out,
    X, T, TT, XX, TI, CB, C, IS, ISM, IM, IG, BM, BV, LM, L,
    local_sem, t_s, t_r, z_s, z_r, f_s, f_r, r_s, r_r, is_s, is_r, ig_s, ig_r,
    cos_s, cos_r, b_s, b_r, l_s, l_r,
):
    Z = S // 2
    n, width = src.shape[0], tgt.shape[0]
    half = n * Z
    height = n * S
    HF, HR = G // 2, (G - 1) // 2
    g, s = lax.axis_index("grp"), lax.axis_index("shard")
    c, z = lax.rem(s, 2), s // 2
    sgn = 1 - 2 * c
    odd = lax.rem(g, 2)
    p = (1 - odd) * (g // 2) + odd * (G - 1 - g // 2)

    def at(r):
        q = lax.rem(p + sgn * r + G, G)
        h = q // (G // 2)
        return (1 - h) * 2 * q + h * (2 * (G - 1 - q) + 1)

    ahead = [at(r) for r in range(G)]
    order = [0]
    for r in range(1, HF + 1):
        order += [G - r] if G - r == r else [G - r, r]
    zs = [z] + [jnp.bitwise_xor(z, k) for k in range(1, Z)]
    other = 1 - c
    sib = z * 2 + other

    def rows(k):
        return pl.ds(pl.multiple_of(zs[k] * n, n), n)

    def send(a, b, ss, rs, dev):
        cp = pltpu.make_async_remote_copy(a, b, ss, rs, device_id=dev, device_id_type=MESH)
        cp.start()
        sends.append(cp)

    def arrived(b, rs):
        pltpu.make_async_copy(b, b, rs).wait()

    def signal(dev):
        pl.semaphore_signal(barrier, inc=1, device_id=dev, device_id_type=MESH)

    sends = []
    barrier = pltpu.get_barrier_semaphore()
    for r in range(G):
        for d in range(S):
            if (r, d) != (0, 0):
                signal((ahead[r], lax.rem(s + d, S)))
    mine_t = pl.ds(pl.multiple_of(c * width, width), width)
    tcopy = pltpu.make_async_copy(tgt, T.at[mine_t, :], local_sem.at[0])
    tcopy.start()
    scopy = pltpu.make_async_copy(src, X.at[g, rows(0), :], local_sem.at[1])
    scopy.start()
    TI[c] = jnp.broadcast_to(inv_tgt[...], (8, width))
    pl.semaphore_wait(barrier, G * S - 1)

    for k in range(1, Z):
        send(src, X.at[g, rows(0), :], z_s.at[k], z_r.at[k], (g, zs[k] * 2 + c))

    fwd, back = (ahead[1], s), (ahead[G - 1], s)

    def onward(piece, where, k, hop, stream):
        if stream != "r" and hop < HF:
            send(piece, where, f_s.at[hop, k], f_r.at[hop, k], fwd)
        if stream != "f" and hop < HR:
            send(piece, where, r_s.at[hop, k], r_r.at[hop, k], back)

    def prepare(r, k):
        high, low = split(X[ahead[r], rows(k), :])
        i = order.index(r)
        XX[i, rows(k), :] = high
        XX[i, pl.ds(pl.multiple_of(half + zs[k] * n, n), n), :] = low

    wide = L.shape[3]

    def lying(x):
        x = jnp.broadcast_to(x, (half, 128))
        return jnp.transpose(jnp.concatenate([x] * (wide // half), axis=0))[:8, :]

    def standing(x):
        return jnp.transpose(jnp.broadcast_to(x, (128, wide)))[:half, :]

    def row_sums(r, parts):
        if r == 0:
            inv = IS[c]
        else:
            arrived(IG.at[ahead[r]], ig_r.at[G - r])
            inv = standing(IG[ahead[r], 0:1, :])
        logits = [x * inv for x in parts]
        top = jnp.max(jnp.maximum(logits[0], logits[1]), axis=1, keepdims=True)
        total = jnp.sum(
            jnp.exp(logits[0] - top) + jnp.exp(logits[1] - top), axis=1, keepdims=True
        )
        LM[r] = lying(top + jnp.log(total))
        where = L.at[c, z * G + g]
        for d in range(S):
            if (r, d) == (0, 0):
                L[c, z * G + g] = LM[0]
            else:
                send(
                    LM.at[r], where, l_s.at[r, d], l_r.at[r, d],
                    (ahead[r], lax.rem(s + d, S)),
                )

    state = [None, None]

    def column(o, cos):
        logits = cos * TI[o, 0:1, :]
        top = jnp.max(logits, axis=0, keepdims=True)
        if state[o] is not None:
            top = jnp.maximum(top, state[o][0])
        total = jnp.sum(jnp.exp(logits - top), axis=0, keepdims=True)
        if state[o] is not None:
            total = total + state[o][1] * jnp.exp(state[o][0] - top)
        state[o] = (top, total)

    def finish(first, last):
        count = last - first
        w = lax.dot_general(
            XX[first:last].reshape(count * 2 * half, XX.shape[2]), TT[...],
            (((1,), (1,)), ((), ())), preferred_element_type=jnp.float32,
        ).reshape(count, 2 * half, 4 * width)
        blocks = []
        for i in range(count):
            r, v = order[first + i], w[i]
            cos = v[:half, : 2 * width] + (v[:half, 2 * width :] + v[half:, : 2 * width])
            parts = [cos[:, o * width : (o + 1) * width] for o in range(2)]
            blocks.append(parts)
            for o in range(2):
                CB[r, o] = parts[o]
                if r > 0:
                    send(
                        CB.at[r, o], C.at[g, c], cos_s.at[r, o], cos_r.at[r, c],
                        (ahead[r], z * 2 + o),
                    )
            if r == 0:
                C[g, c] = CB[0, c]
                send(CB.at[0, other], C.at[g, c], cos_s.at[0, 0], cos_r.at[0, c], (g, sib))
        for i, parts in enumerate(blocks):
            row_sums(order[first + i], parts)
        for parts in blocks:
            for o in range(2):
                column(o, parts[o])

    chunk = width // 4

    def piece_of(o, i):
        return pl.ds(pl.multiple_of(o * width + i * chunk, chunk), chunk)

    def targets(o, i):
        high, low = split(T[piece_of(o, i), :])
        TT[piece_of(o, i), :] = high
        TT[piece_of(o + 2, i), :] = low

    finished = 0
    for t in range(Z + HF):
        ready = []
        for h in range(HF, -1, -1):
            k = t - h
            if not 0 <= k < Z:
                continue
            if h == 0:
                where = X.at[g, rows(k), :]
                if k == 0:
                    onward(src, where, 0, 0, "own")
                else:
                    arrived(where, z_r.at[k])
                    onward(where, where, k, 0, "own")
                    ready.append((0, k))
                continue
            where = X.at[ahead[G - h], rows(k), :]
            arrived(where, f_r.at[h - 1, k])
            onward(where, where, k, h, "f")
            ready.append((G - h, k))
            if h <= HR:
                where = X.at[ahead[h], rows(k), :]
                arrived(where, r_r.at[h - 1, k])
                onward(where, where, k, h, "r")
                ready.append((h, k))
        if t < 4:
            send(
                tgt.at[pl.ds(t * chunk, chunk), :], T.at[piece_of(c, t), :],
                t_s.at[t], t_r.at[t], (g, sib),
            )
        if t == 0:
            send(TI.at[c], TI.at[c], t_s.at[4], t_r.at[4], (g, sib))
            lane = lax.broadcasted_iota(jnp.int32, (n, n), 1)
            sub = lax.broadcasted_iota(jnp.int32, (n, n), 0)
            column_inv = jnp.sum(
                jnp.where(lane == sub, jnp.broadcast_to(inv_src[...], (n, n)), 0.0),
                axis=1, keepdims=True,
            )
            ISM[...] = jnp.broadcast_to(column_inv, (n, 128))
            IS[c, rows(0), :] = ISM[...]
            for d in range(1, S):
                send(ISM, IS.at[c, rows(0), :], is_s.at[d], is_r.at[d], (g, lax.rem(s + d, S)))
            scopy.wait()
            prepare(0, 0)
            tcopy.wait()
            for i in range(4):
                targets(c, i)
        for r, k in ready:
            prepare(r, k)
        if 1 <= t <= 4:
            arrived(T.at[piece_of(other, t - 1), :], t_r.at[t - 1])
            targets(other, t - 1)
        if t == 4:
            arrived(TI.at[other], t_r.at[4])
        if t == 1:
            for d in range(1, S):
                frm = lax.rem(s + S - d, S)
                place = pl.ds(pl.multiple_of(frm // 2 * n, n), n)
                arrived(IS.at[lax.rem(frm, 2), place, :], is_r.at[d])
            IM[...] = lying(IS[c])
            for r in range(1, G):
                send(IM, IG.at[g], ig_s.at[r], ig_r.at[r], (ahead[r], s))
        if t >= Z:
            done = len([r for r, k in ready if k == Z - 1])
            finish(finished, finished + done + (t == Z))
            finished += done + (t == Z)

    for o in range(2):
        top, total = state[o]
        BM[o] = TI[o]
        BM[o, 0:1, :] = top + jnp.log(total)
    BV[g, c] = BM[c]
    send(BM.at[other], BV.at[g, c], b_s.at[0, 0], b_r.at[0, c], (g, sib))
    for r in range(1, G):
        for o in range(2):
            send(BM.at[o], BV.at[g, c], b_s.at[r, o], b_r.at[r, c], (ahead[r], z * 2 + o))

    froms = [(g, other, 0)]
    for r in range(1, G):
        froms += [(ahead[G - r], c, r), (ahead[r], other, r)]
    for group, core, r in froms:
        arrived(C.at[group, core], cos_r.at[r, core])

    inv_rows = IS[...]
    for group, core, r in froms:
        arrived(BV.at[group, core], b_r.at[r, core])
    for d in range(S):
        frm = lax.rem(s + S - d, S)
        for r in range(G):
            if (r, d) != (0, 0):
                group = ahead[(G - r) % G] if d % 2 == 0 else ahead[r]
                arrived(L.at[lax.rem(frm, 2), frm // 2 * G + group], l_r.at[r, d])

    a = []
    for o in range(2):
        parts = L[o]
        top = jnp.max(parts, axis=0)
        total = jnp.sum(jnp.exp(parts - top[None]), axis=0)
        a.append(standing((top + jnp.log(total) - math.log(G * width * S))[:1, :]))
    a = jnp.stack(a)
    for j in range(G):
        first, second = BV[j, 0, 0:1, :], BV[j, 1, 0:1, :]
        b = jnp.maximum(first, second) + jnp.log(1.0 + jnp.exp(-jnp.abs(first - second)))
        b = b - math.log(height * G)
        both = jnp.maximum(a, b) + jnp.log(1.0 + jnp.exp(-jnp.abs(a - b)))
        scale = 0.5 * (inv_rows + BV[j, 0, 1:2, :])
        margin = C[j] * scale - (both - math.log(2.0))
        for o in range(2):
            for q in range(Z):
                place = (q * 2 + o) * n
                out[place : place + n, j * width : (j + 1) * width] = margin[o, q * n : (q + 1) * n]

    for cp in sends:
        cp.wait_send()


def body(src, inv_src, tgt, inv_tgt):
    G, S = lax.axis_size("grp"), lax.axis_size("shard")
    n, depth = src.shape
    width = tgt.shape[0]
    height = n * S
    half = height // 2
    wide = max(half, 128)
    Z, HF, HR = S // 2, G // 2, (G - 1) // 2
    f32, bf16 = jnp.float32, jnp.bfloat16
    dma = pltpu.SemaphoreType.DMA
    vmem = pl.BlockSpec(memory_space=pltpu.VMEM)
    anyw = pl.BlockSpec(memory_space=pl.ANY)
    return pl.pallas_call(
        functools.partial(kernel, G, S),
        out_shape=jax.ShapeDtypeStruct((height, G * width), f32),
        in_specs=[anyw, vmem, anyw, vmem],
        out_specs=vmem,
        scratch_shapes=[
            pltpu.VMEM((G, half, depth), f32),
            pltpu.VMEM((2 * width, depth), f32),
            pltpu.VMEM((4 * width, depth), bf16),
            pltpu.VMEM((G, 2 * half, depth), bf16),
            pltpu.VMEM((2, 8, width), f32),
            pltpu.VMEM((G, 2, half, width), f32),
            pltpu.VMEM((G, 2, half, width), f32),
            pltpu.VMEM((2, half, 128), f32),
            pltpu.VMEM((n, 128), f32),
            pltpu.VMEM((8, wide), f32),
            pltpu.VMEM((G, 8, wide), f32),
            pltpu.VMEM((2, 8, width), f32),
            pltpu.VMEM((G, 2, 8, width), f32),
            pltpu.VMEM((G, 8, wide), f32),
            pltpu.VMEM((2, Z * G, 8, wide), f32),
            dma((2,)),
            dma((5,)), dma((5,)),
            dma((Z,)), dma((Z,)),
            dma((HF, Z)), dma((HF, Z)),
            dma((HR, Z)), dma((HR, Z)),
            dma((S,)), dma((S,)),
            dma((G,)), dma((G,)),
            dma((G, 2)), dma((G, 2)),
            dma((G, 2)), dma((G, 2)),
            dma((G, S)), dma((G, S)),
        ],
        compiler_params=pltpu.CompilerParams(
            collective_id=0, has_side_effects=True, vmem_limit_bytes=56 * 2**20
        ),
        cost_estimate=pl.CostEstimate(
            flops=8 * G * height * width * depth, bytes_accessed=8 * width * depth,
            transcendentals=4 * G * height * width,
        ),
    )(src, inv_src.reshape(1, n), tgt, inv_tgt.reshape(1, width))


def solution(mesh):
    return jax.shard_map(
        body,
        mesh=mesh,
        in_specs=(
            P(("grp", "shard"), None),
            P(("grp", "shard")),
            P(("shard", "grp"), None),
            P(("shard", "grp")),
        ),
        out_specs=P("grp", "shard"),
        check_vma=False,
    )
```

```python
import functools
import math

import jax
import jax.numpy as jnp
from jax import lax
from jax.experimental import pallas as pl
from jax.experimental.pallas import tpu as pltpu
from jax.sharding import PartitionSpec as P

MESH = pl.DeviceIdType.MESH


def split(rows):
    unit = rows * lax.rsqrt(jnp.sum(rows * rows, axis=1, keepdims=True) + 1e-06)
    high = unit.astype(jnp.bfloat16)
    return high, (unit - high.astype(jnp.float32)).astype(jnp.bfloat16)


def kernel(
    G, S, src, inv_src, tgt, inv_tgt, out,
    X, T, TT, XX, TI, CB, C, IS, ISM, BM, BV, LM, L,
    local_sem, t_s, t_r, z_s, z_r, f_s, f_r, r_s, r_r, is_s, is_r,
    cos_s, cos_r, b_s, b_r, l_s, l_r,
):
    Z = S // 2
    n, width = src.shape[0], tgt.shape[0]
    half = n * Z
    height = n * S
    HF, HR = G // 2, (G - 1) // 2
    g, s = lax.axis_index("grp"), lax.axis_index("shard")
    c, z = lax.rem(s, 2), s // 2
    sgn = 1 - 2 * c
    odd = lax.rem(g, 2)
    p = (1 - odd) * (g // 2) + odd * (G - 1 - g // 2)

    def at(r):
        q = lax.rem(p + sgn * r + G, G)
        h = q // (G // 2)
        return (1 - h) * 2 * q + h * (2 * (G - 1 - q) + 1)

    ahead = [at(r) for r in range(G)]
    order = [0]
    for r in range(1, HF + 1):
        order += [G - r] if G - r == r else [G - r, r]
    low_half = jnp.where(z < Z // 2, 1, 0)
    near = low_half * z + (1 - low_half) * (Z - 1 - z)
    toward = 2 * low_half - 1

    def nearest(k):
        both = z + toward * ((k + 1) // 2) if k % 2 else z - toward * (k // 2)
        return jnp.where(k <= 2 * near, both, low_half * k + (1 - low_half) * (Z - 1 - k))

    zs = [z] + [nearest(k) for k in range(1, Z)]
    other = 1 - c
    sib = z * 2 + other

    def rows(k):
        return pl.ds(pl.multiple_of(zs[k] * n, n), n)

    def send(a, b, ss, rs, dev):
        cp = pltpu.make_async_remote_copy(a, b, ss, rs, device_id=dev, device_id_type=MESH)
        cp.start()
        sends.append(cp)

    def arrived(b, rs):
        pltpu.make_async_copy(b, b, rs).wait()

    def signal(dev):
        pl.semaphore_signal(barrier, inc=1, device_id=dev, device_id_type=MESH)

    sends = []
    barrier = pltpu.get_barrier_semaphore()
    for d in range(1, S):
        signal((g, lax.rem(s + d, S)))
    for r in range(1, G):
        for o in range(2):
            signal((ahead[r], z * 2 + o))
    mine_t = pl.ds(pl.multiple_of(c * width, width), width)
    tcopy = pltpu.make_async_copy(tgt, T.at[mine_t, :], local_sem.at[0])
    tcopy.start()
    scopy = pltpu.make_async_copy(src, X.at[g, rows(0), :], local_sem.at[1])
    scopy.start()
    TI[c] = jnp.broadcast_to(inv_tgt[...], (8, width))
    pl.semaphore_wait(barrier, S - 1 + 2 * (G - 1))

    late = []

    def along(piece, where, at_z, step, go):
        cp = pltpu.make_async_remote_copy(
            piece, where, z_s.at[(step + 1) // 2, at_z], z_r.at[at_z],
            device_id=(g, lax.rem(z + step + Z, Z) * 2 + c), device_id_type=MESH,
        )
        pl.when(go)(cp.start)
        late.append((go, cp))

    for step in (-1, 1):
        there = z + step
        along(src, X.at[g, rows(0), :], z, step, (there >= 0) & (there < Z))

    fwd, back = (ahead[1], s), (ahead[G - 1], s)

    def onward(piece, where, k, hop, stream):
        if stream != "r" and hop < HF:
            send(piece, where, f_s.at[hop, k], f_r.at[hop, k], fwd)
        if stream != "f" and hop < HR:
            send(piece, where, r_s.at[hop, k], r_r.at[hop, k], back)

    def prepare(r, k):
        high, low = split(X[ahead[r], rows(k), :])
        i = order.index(r)
        XX[i, rows(k), :] = high
        XX[i, pl.ds(pl.multiple_of(half + zs[k] * n, n), n), :] = low

    state = [None, None]

    def column(o, cos):
        logits = cos * TI[o, 0:1, :]
        top = jnp.max(logits, axis=0, keepdims=True)
        if state[o] is not None:
            top = jnp.maximum(top, state[o][0])
        total = jnp.sum(jnp.exp(logits - top), axis=0, keepdims=True)
        if state[o] is not None:
            total = total + state[o][1] * jnp.exp(state[o][0] - top)
        state[o] = (top, total)

    def finish(first, last):
        count = last - first
        w = lax.dot_general(
            XX[first:last].reshape(count * 2 * half, XX.shape[2]), TT[...],
            (((1,), (1,)), ((), ())), preferred_element_type=jnp.float32,
        ).reshape(count, 2 * half, 4 * width)
        blocks = []
        for i in range(count):
            r, v = order[first + i], w[i]
            cos = v[:half, : 2 * width] + (v[:half, 2 * width :] + v[half:, : 2 * width])
            parts = [cos[:, o * width : (o + 1) * width] for o in range(2)]
            blocks.append(parts)
            for o in range(2):
                CB[r, o] = parts[o]
                if r > 0:
                    send(
                        CB.at[r, o], C.at[g, c], cos_s.at[r, o], cos_r.at[r, c],
                        (ahead[r], z * 2 + o),
                    )
            if r == 0:
                C[g, c] = CB[0, c]
                send(CB.at[0, other], C.at[g, c], cos_s.at[0, 0], cos_r.at[0, c], (g, sib))
        for parts in blocks:
            for o in range(2):
                column(o, parts[o])

    chunk = width // 4

    def piece_of(o, i):
        return pl.ds(pl.multiple_of(o * width + i * chunk, chunk), chunk)

    def targets(o, i):
        high, low = split(T[piece_of(o, i), :])
        TT[piece_of(o, i), :] = high
        TT[piece_of(o + 2, i), :] = low

    finished = 0
    for t in range(Z + HF):
        ready = []
        for h in range(HF + 1):
            k = t - h
            if not 0 <= k < Z:
                continue
            if h == 0:
                where = X.at[g, rows(k), :]
                if k == 0:
                    onward(src, where, 0, 0, "own")
                else:
                    arrived(where, z_r.at[zs[k]])
                    along(where, where, zs[k], 1, (zs[k] < z) & (z + 1 < Z))
                    along(where, where, zs[k], -1, (zs[k] > z) & (z >= 1))
                    onward(where, where, k, 0, "own")
                    ready.append((0, k))
                continue
            where = X.at[ahead[G - h], rows(k), :]
            arrived(where, f_r.at[h - 1, k])
            onward(where, where, k, h, "f")
            ready.append((G - h, k))
            if h <= HR:
                where = X.at[ahead[h], rows(k), :]
                arrived(where, r_r.at[h - 1, k])
                onward(where, where, k, h, "r")
                ready.append((h, k))
        if t < 4:
            send(
                tgt.at[pl.ds(t * chunk, chunk), :], T.at[piece_of(c, t), :],
                t_s.at[t], t_r.at[t], (g, sib),
            )
        if t == 0:
            send(TI.at[c], TI.at[c], t_s.at[4], t_r.at[4], (g, sib))
            lane = lax.broadcasted_iota(jnp.int32, (n, n), 1)
            sub = lax.broadcasted_iota(jnp.int32, (n, n), 0)
            column_inv = jnp.sum(
                jnp.where(lane == sub, jnp.broadcast_to(inv_src[...], (n, n)), 0.0),
                axis=1, keepdims=True,
            )
            ISM[...] = jnp.broadcast_to(column_inv, (n, 128))
            IS[c, rows(0), :] = ISM[...]
            for d in range(1, S):
                send(ISM, IS.at[c, rows(0), :], is_s.at[d], is_r.at[d], (g, lax.rem(s + d, S)))
            scopy.wait()
            prepare(0, 0)
            tcopy.wait()
            for i in range(4):
                targets(c, i)
        for r, k in ready:
            prepare(r, k)
        if 1 <= t <= 4:
            arrived(T.at[piece_of(other, t - 1), :], t_r.at[t - 1])
            targets(other, t - 1)
        if t == 4:
            arrived(TI.at[other], t_r.at[4])
        if t >= Z:
            done = len([r for r, k in ready if k == Z - 1])
            finish(finished, finished + done + (t == Z))
            finished += done + (t == Z)

    for o in range(2):
        top, total = state[o]
        BM[o] = TI[o]
        BM[o, 0:1, :] = top + jnp.log(total)
    BV[g, c] = BM[c]
    send(BM.at[other], BV.at[g, c], b_s.at[0, 0], b_r.at[0, c], (g, sib))
    for r in range(1, G):
        for o in range(2):
            send(BM.at[o], BV.at[g, c], b_s.at[r, o], b_r.at[r, c], (ahead[r], z * 2 + o))

    for d in range(1, S):
        frm = lax.rem(s + S - d, S)
        place = pl.ds(pl.multiple_of(frm // 2 * n, n), n)
        arrived(IS.at[lax.rem(frm, 2), place, :], is_r.at[d])

    froms = [(g, other, 0)]
    for r in range(1, G):
        froms += [(ahead[G - r], c, r), (ahead[r], other, r)]
    for group, core, r in froms:
        arrived(C.at[group, core], cos_r.at[r, core])

    inv_rows = IS[...]
    logits = [C[j] * inv_rows for j in range(G)]
    top = jnp.max(functools.reduce(jnp.maximum, logits), axis=2, keepdims=True)
    total = jnp.sum(sum(jnp.exp(x - top) for x in logits), axis=2, keepdims=True)
    part = (top + jnp.log(total)).reshape(height, 1)
    LM[...] = jnp.transpose(jnp.broadcast_to(part, (height, 128)))[:8, :]
    L[s] = LM[...]
    for d in range(1, S):
        send(LM, L.at[s], l_s.at[d], l_r.at[d], (g, lax.rem(s + d, S)))
    for group, core, r in froms:
        arrived(BV.at[group, core], b_r.at[r, core])
    for d in range(1, S):
        arrived(L.at[lax.rem(s + S - d, S)], l_r.at[d])

    parts = L[...]
    top = jnp.max(parts, axis=0)
    a = top + jnp.log(jnp.sum(jnp.exp(parts - top[None]), axis=0)) - math.log(G * width * S)
    a = jnp.transpose(jnp.broadcast_to(a[:1, :], (128, height))).reshape(2, half, 128)
    for j in range(G):
        first, second = BV[j, 0, 0:1, :], BV[j, 1, 0:1, :]
        b = jnp.maximum(first, second) + jnp.log(1.0 + jnp.exp(-jnp.abs(first - second)))
        b = b - math.log(height * G)
        both = jnp.maximum(a, b) + jnp.log(1.0 + jnp.exp(-jnp.abs(a - b)))
        scale = 0.5 * (inv_rows + BV[j, 0, 1:2, :])
        margin = C[j] * scale - (both - math.log(2.0))
        for o in range(2):
            for q in range(Z):
                place = (q * 2 + o) * n
                out[place : place + n, j * width : (j + 1) * width] = margin[o, q * n : (q + 1) * n]

    for cp in sends:
        cp.wait_send()
    for go, cp in late:
        pl.when(go)(cp.wait_send)


def body(src, inv_src, tgt, inv_tgt):
    G, S = lax.axis_size("grp"), lax.axis_size("shard")
    n, depth = src.shape
    width = tgt.shape[0]
    height = n * S
    half = height // 2
    Z, HF, HR = S // 2, G // 2, (G - 1) // 2
    f32, bf16 = jnp.float32, jnp.bfloat16
    dma = pltpu.SemaphoreType.DMA
    vmem = pl.BlockSpec(memory_space=pltpu.VMEM)
    anyw = pl.BlockSpec(memory_space=pl.ANY)
    return pl.pallas_call(
        functools.partial(kernel, G, S),
        out_shape=jax.ShapeDtypeStruct((height, G * width), f32),
        in_specs=[anyw, vmem, anyw, vmem],
        out_specs=vmem,
        scratch_shapes=[
            pltpu.VMEM((G, half, depth), f32),
            pltpu.VMEM((2 * width, depth), f32),
            pltpu.VMEM((4 * width, depth), bf16),
            pltpu.VMEM((G, 2 * half, depth), bf16),
            pltpu.VMEM((2, 8, width), f32),
            pltpu.VMEM((G, 2, half, width), f32),
            pltpu.VMEM((G, 2, half, width), f32),
            pltpu.VMEM((2, half, 128), f32),
            pltpu.VMEM((n, 128), f32),
            pltpu.VMEM((2, 8, width), f32),
            pltpu.VMEM((G, 2, 8, width), f32),
            pltpu.VMEM((8, height), f32),
            pltpu.VMEM((S, 8, height), f32),
            dma((2,)),
            dma((5,)), dma((5,)),
            dma((2, Z)), dma((Z,)),
            dma((HF, Z)), dma((HF, Z)),
            dma((HR, Z)), dma((HR, Z)),
            dma((S,)), dma((S,)),
            dma((G, 2)), dma((G, 2)),
            dma((G, 2)), dma((G, 2)),
            dma((S,)), dma((S,)),
        ],
        compiler_params=pltpu.CompilerParams(
            collective_id=0, has_side_effects=True, vmem_limit_bytes=56 * 2**20
        ),
        cost_estimate=pl.CostEstimate(
            flops=8 * G * height * width * depth, bytes_accessed=8 * width * depth,
            transcendentals=4 * G * height * width,
        ),
    )(src, inv_src.reshape(1, n), tgt, inv_tgt.reshape(1, width))


def solution(mesh):
    return jax.shard_map(
        body,
        mesh=mesh,
        in_specs=(
            P(("grp", "shard"), None),
            P(("grp", "shard")),
            P(("shard", "grp"), None),
            P(("shard", "grp")),
        ),
        out_specs=P("grp", "shard"),
        check_vma=False,
    )
```

```python
import functools
import math

import jax
import jax.numpy as jnp
from jax import lax
from jax.experimental import pallas as pl
from jax.experimental.pallas import tpu as pltpu
from jax.sharding import PartitionSpec as P

MESH = pl.DeviceIdType.MESH


def split(rows):
    unit = rows * lax.rsqrt(jnp.sum(rows * rows, axis=1, keepdims=True) + 1e-06)
    high = unit.astype(jnp.bfloat16)
    return high, (unit - high.astype(jnp.float32)).astype(jnp.bfloat16)


def kernel(
    G, S, src, inv_src, tgt, inv_tgt, out,
    X, T, TT, XX, TI, CB, C, IS, ISM, BM, BV, LM, L,
    local_sem, t_s, t_r, z_s, z_r, f_s, f_r, r_s, r_r, is_s, is_r,
    cos_s, cos_r, b_s, b_r, l_s, l_r,
):
    Z = S // 2
    n, width = src.shape[0], tgt.shape[0]
    half = n * Z
    height = n * S
    HF, HR = G // 2, (G - 1) // 2
    g, s = lax.axis_index("grp"), lax.axis_index("shard")
    c, z = lax.rem(s, 2), s // 2
    sgn = 1 - 2 * c
    odd = lax.rem(g, 2)
    p = (1 - odd) * (g // 2) + odd * (G - 1 - g // 2)

    def at(r):
        q = lax.rem(p + sgn * r + G, G)
        h = q // (G // 2)
        return (1 - h) * 2 * q + h * (2 * (G - 1 - q) + 1)

    ahead = [at(r) for r in range(G)]
    order = [0]
    for r in range(1, HF + 1):
        order += [G - r] if G - r == r else [G - r, r]
    low_half = jnp.where(z < Z // 2, 1, 0)
    near = low_half * z + (1 - low_half) * (Z - 1 - z)
    toward = 2 * low_half - 1

    def nearest(k):
        both = z + toward * ((k + 1) // 2) if k % 2 else z - toward * (k // 2)
        return jnp.where(k <= 2 * near, both, low_half * k + (1 - low_half) * (Z - 1 - k))

    zs = [z] + [nearest(k) for k in range(1, Z)]
    other = 1 - c
    sib = z * 2 + other

    def rows(k):
        return pl.ds(pl.multiple_of(zs[k] * n, n), n)

    def send(a, b, ss, rs, dev):
        cp = pltpu.make_async_remote_copy(a, b, ss, rs, device_id=dev, device_id_type=MESH)
        cp.start()
        sends.append(cp)

    def arrived(b, rs):
        pltpu.make_async_copy(b, b, rs).wait()

    def signal(dev):
        pl.semaphore_signal(barrier, inc=1, device_id=dev, device_id_type=MESH)

    sends = []
    barrier = pltpu.get_barrier_semaphore()
    for d in range(1, S):
        signal((g, lax.rem(s + d, S)))
    for r in range(1, G):
        for o in range(2):
            signal((ahead[r], z * 2 + o))
    mine_t = pl.ds(pl.multiple_of(c * width, width), width)
    tcopy = pltpu.make_async_copy(tgt, T.at[mine_t, :], local_sem.at[0])
    tcopy.start()
    scopy = pltpu.make_async_copy(src, X.at[g, rows(0), :], local_sem.at[1])
    scopy.start()
    TI[c] = jnp.broadcast_to(inv_tgt[...], (8, width))
    pl.semaphore_wait(barrier, S - 1 + 2 * (G - 1))

    late = []

    def along(piece, where, at_z, step, go):
        cp = pltpu.make_async_remote_copy(
            piece, where, z_s.at[(step + 1) // 2, at_z], z_r.at[at_z],
            device_id=(g, lax.rem(z + step + Z, Z) * 2 + c), device_id_type=MESH,
        )
        pl.when(go)(cp.start)
        late.append((go, cp))

    for step in (-1, 1):
        there = z + step
        along(src, X.at[g, rows(0), :], z, step, (there >= 0) & (there < Z))

    fwd, back = (ahead[1], s), (ahead[G - 1], s)

    def onward(piece, where, k, hop, stream):
        if stream != "r" and hop < HF:
            send(piece, where, f_s.at[hop, k], f_r.at[hop, k], fwd)
        if stream != "f" and hop < HR:
            send(piece, where, r_s.at[hop, k], r_r.at[hop, k], back)

    def prepare(r, k):
        high, low = split(X[ahead[r], rows(k), :])
        i = order.index(r)
        XX[i, rows(k), :] = high
        XX[i, pl.ds(pl.multiple_of(half + zs[k] * n, n), n), :] = low

    state = [None, None]

    def column(o, cos):
        logits = cos * TI[o, 0:1, :]
        top = jnp.max(logits, axis=0, keepdims=True)
        if state[o] is not None:
            top = jnp.maximum(top, state[o][0])
        total = jnp.sum(jnp.exp(logits - top), axis=0, keepdims=True)
        if state[o] is not None:
            total = total + state[o][1] * jnp.exp(state[o][0] - top)
        state[o] = (top, total)

    def finish(first, last):
        count = last - first
        w = lax.dot_general(
            XX[first:last].reshape(count * 2 * half, XX.shape[2]), TT[...],
            (((1,), (1,)), ((), ())), preferred_element_type=jnp.float32,
        ).reshape(count, 2 * half, 4 * width)
        blocks = []
        for i in range(count):
            r, v = order[first + i], w[i]
            cos = v[:half, : 2 * width] + (v[:half, 2 * width :] + v[half:, : 2 * width])
            parts = [cos[:, o * width : (o + 1) * width] for o in range(2)]
            blocks.append(parts)
            for o in range(2):
                CB[r, o] = parts[o]
                if r > 0:
                    send(
                        CB.at[r, o], C.at[g, c], cos_s.at[r, o], cos_r.at[r, c],
                        (ahead[r], z * 2 + o),
                    )
            if r == 0:
                C[g, c] = CB[0, c]
                send(CB.at[0, other], C.at[g, c], cos_s.at[0, 0], cos_r.at[0, c], (g, sib))
        for parts in blocks:
            for o in range(2):
                column(o, parts[o])

    chunk = width // 4

    def piece_of(o, i):
        return pl.ds(pl.multiple_of(o * width + i * chunk, chunk), chunk)

    def targets(o, i):
        high, low = split(T[piece_of(o, i), :])
        TT[piece_of(o, i), :] = high
        TT[piece_of(o + 2, i), :] = low

    finished = 0
    for t in range(Z + HF):
        ready = []
        for h in range(HF + 1):
            k = t - h
            if not 0 <= k < Z:
                continue
            if h == 0:
                where = X.at[g, rows(k), :]
                if k == 0:
                    onward(src, where, 0, 0, "own")
                else:
                    arrived(where, z_r.at[zs[k]])
                    along(where, where, zs[k], 1, (zs[k] < z) & (z + 1 < Z))
                    along(where, where, zs[k], -1, (zs[k] > z) & (z >= 1))
                    onward(where, where, k, 0, "own")
                    ready.append((0, k))
                continue
            where = X.at[ahead[G - h], rows(k), :]
            arrived(where, f_r.at[h - 1, k])
            onward(where, where, k, h, "f")
            ready.append((G - h, k))
            if h <= HR:
                where = X.at[ahead[h], rows(k), :]
                arrived(where, r_r.at[h - 1, k])
                onward(where, where, k, h, "r")
                ready.append((h, k))
        if t < 4:
            send(
                tgt.at[pl.ds(t * chunk, chunk), :], T.at[piece_of(c, t), :],
                t_s.at[t], t_r.at[t], (g, sib),
            )
        if t == 0:
            send(TI.at[c], TI.at[c], t_s.at[4], t_r.at[4], (g, sib))
        if t == 1:
            tcopy.wait()
            scopy.wait()
            ready.append((0, 0))
        if 1 <= t <= 4:
            targets(c, t - 1)
        if t == 2:
            lane = lax.broadcasted_iota(jnp.int32, (n, n), 1)
            sub = lax.broadcasted_iota(jnp.int32, (n, n), 0)
            column_inv = jnp.sum(
                jnp.where(lane == sub, jnp.broadcast_to(inv_src[...], (n, n)), 0.0),
                axis=1, keepdims=True,
            )
            ISM[...] = jnp.broadcast_to(column_inv, (n, 128))
            IS[c, rows(0), :] = ISM[...]
            for d in range(1, S):
                send(ISM, IS.at[c, rows(0), :], is_s.at[d], is_r.at[d], (g, lax.rem(s + d, S)))
        for r, k in ready:
            prepare(r, k)
        if 1 <= t <= 4:
            arrived(T.at[piece_of(other, t - 1), :], t_r.at[t - 1])
            targets(other, t - 1)
        if t == 4:
            arrived(TI.at[other], t_r.at[4])
        if t >= Z:
            done = len([r for r, k in ready if k == Z - 1])
            finish(finished, finished + done + (t == Z))
            finished += done + (t == Z)

    for o in range(2):
        top, total = state[o]
        BM[o] = TI[o]
        BM[o, 0:1, :] = top + jnp.log(total)
    BV[g, c] = BM[c]
    send(BM.at[other], BV.at[g, c], b_s.at[0, 0], b_r.at[0, c], (g, sib))
    for r in range(1, G):
        for o in range(2):
            send(BM.at[o], BV.at[g, c], b_s.at[r, o], b_r.at[r, c], (ahead[r], z * 2 + o))

    for d in range(1, S):
        frm = lax.rem(s + S - d, S)
        place = pl.ds(pl.multiple_of(frm // 2 * n, n), n)
        arrived(IS.at[lax.rem(frm, 2), place, :], is_r.at[d])

    froms = [(g, other, 0)]
    for r in range(1, G):
        froms += [(ahead[G - r], c, r), (ahead[r], other, r)]
    for group, core, r in froms:
        arrived(C.at[group, core], cos_r.at[r, core])

    inv_rows = IS[...]
    logits = [C[j] * inv_rows for j in range(G)]
    top = jnp.max(functools.reduce(jnp.maximum, logits), axis=2, keepdims=True)
    total = jnp.sum(sum(jnp.exp(x - top) for x in logits), axis=2, keepdims=True)
    part = (top + jnp.log(total)).reshape(height, 1)
    LM[...] = jnp.transpose(jnp.broadcast_to(part, (height, 128)))[:8, :]
    L[s] = LM[...]
    for d in range(1, S):
        send(LM, L.at[s], l_s.at[d], l_r.at[d], (g, lax.rem(s + d, S)))
    for group, core, r in froms:
        arrived(BV.at[group, core], b_r.at[r, core])
    for d in range(1, S):
        arrived(L.at[lax.rem(s + S - d, S)], l_r.at[d])

    parts = L[...]
    top = jnp.max(parts, axis=0)
    a = top + jnp.log(jnp.sum(jnp.exp(parts - top[None]), axis=0)) - math.log(G * width * S)
    a = jnp.transpose(jnp.broadcast_to(a[:1, :], (128, height))).reshape(2, half, 128)
    for j in range(G):
        first, second = BV[j, 0, 0:1, :], BV[j, 1, 0:1, :]
        b = jnp.maximum(first, second) + jnp.log(1.0 + jnp.exp(-jnp.abs(first - second)))
        b = b - math.log(height * G)
        both = jnp.maximum(a, b) + jnp.log(1.0 + jnp.exp(-jnp.abs(a - b)))
        scale = 0.5 * (inv_rows + BV[j, 0, 1:2, :])
        margin = C[j] * scale - (both - math.log(2.0))
        for o in range(2):
            for q in range(Z):
                place = (q * 2 + o) * n
                out[place : place + n, j * width : (j + 1) * width] = margin[o, q * n : (q + 1) * n]

    for cp in sends:
        cp.wait_send()
    for go, cp in late:
        pl.when(go)(cp.wait_send)


def body(src, inv_src, tgt, inv_tgt):
    G, S = lax.axis_size("grp"), lax.axis_size("shard")
    n, depth = src.shape
    width = tgt.shape[0]
    height = n * S
    half = height // 2
    Z, HF, HR = S // 2, G // 2, (G - 1) // 2
    f32, bf16 = jnp.float32, jnp.bfloat16
    dma = pltpu.SemaphoreType.DMA
    vmem = pl.BlockSpec(memory_space=pltpu.VMEM)
    anyw = pl.BlockSpec(memory_space=pl.ANY)
    return pl.pallas_call(
        functools.partial(kernel, G, S),
        out_shape=jax.ShapeDtypeStruct((height, G * width), f32),
        in_specs=[anyw, vmem, anyw, vmem],
        out_specs=vmem,
        scratch_shapes=[
            pltpu.VMEM((G, half, depth), f32),
            pltpu.VMEM((2 * width, depth), f32),
            pltpu.VMEM((4 * width, depth), bf16),
            pltpu.VMEM((G, 2 * half, depth), bf16),
            pltpu.VMEM((2, 8, width), f32),
            pltpu.VMEM((G, 2, half, width), f32),
            pltpu.VMEM((G, 2, half, width), f32),
            pltpu.VMEM((2, half, 128), f32),
            pltpu.VMEM((n, 128), f32),
            pltpu.VMEM((2, 8, width), f32),
            pltpu.VMEM((G, 2, 8, width), f32),
            pltpu.VMEM((8, height), f32),
            pltpu.VMEM((S, 8, height), f32),
            dma((2,)),
            dma((5,)), dma((5,)),
            dma((2, Z)), dma((Z,)),
            dma((HF, Z)), dma((HF, Z)),
            dma((HR, Z)), dma((HR, Z)),
            dma((S,)), dma((S,)),
            dma((G, 2)), dma((G, 2)),
            dma((G, 2)), dma((G, 2)),
            dma((S,)), dma((S,)),
        ],
        compiler_params=pltpu.CompilerParams(
            collective_id=0, has_side_effects=True, vmem_limit_bytes=56 * 2**20
        ),
        cost_estimate=pl.CostEstimate(
            flops=8 * G * height * width * depth, bytes_accessed=8 * width * depth,
            transcendentals=4 * G * height * width,
        ),
    )(src, inv_src.reshape(1, n), tgt, inv_tgt.reshape(1, width))


def solution(mesh):
    return jax.shard_map(
        body,
        mesh=mesh,
        in_specs=(
            P(("grp", "shard"), None),
            P(("grp", "shard")),
            P(("shard", "grp"), None),
            P(("shard", "grp")),
        ),
        out_specs=P("grp", "shard"),
        check_vma=False,
    )
```
